32 devices in a mesh: lp: 2 (over y), col: 4 (over z), row: 2 (over x), sub: 2 (over core).
Axes of the slice: x: 2, y: 2, z: 4, core: 2. Of those that a mesh axis runs over, the one named last changes fastest.
Arguments:
- matrix: bfloat16 [128, 10, 128, 128], P(('lp', 'col', 'row')), parts along dimension 0, may hold values from -0.15625 to 0.15625
- band_cols: int32 [128, 10], P(('lp', 'col', 'row')), parts along dimension 0, may hold values from 0 to 7, as said below
- x_start: float32 [2048, 256], P(('lp', 'col', 'row'), 'sub'), parts along dimension 0, may hold values from -6 to 6
- y_start: float32 [16384, 256], P(('lp', 'col', 'row'), 'sub'), parts along dimension 0, may hold values from 0 to 1
- demand: float32 [16384, 16], P(('lp', 'col', 'row')), parts along dimension 0, may hold values from 0.2 to 24, as said below
- scen_level: int32 [512], P(('lp', 'sub')), parts along dimension 0, may hold values from 0 to 15
- cost: float32 [2048], P(('lp', 'col', 'row')), parts along dimension 0, may hold values from 0.2 to 18, as said below
- upper: float32 [2048], P(('lp', 'col', 'row')), parts along dimension 0, may hold values from 0.2 to 2
- bound_type: int32 [2048], P(('lp', 'col', 'row')), parts along dimension 0, may hold values from 0 to 2
Outputs:
- primal_out: float32 [2048, 256], P(('lp', 'col', 'row'), 'sub'), parts along dimension 0
- dual_out: float32 [16384, 256], P(('lp', 'col', 'row'), 'sub'), parts along dimension 0
- ray_scores: float32 [4, 512], P(None, ('lp', 'sub')), parts along dimension 1
The draws below stay inside these ranges and needn't reach their ends.
There are 2 independent parts, one for each index of `lp`. The reference program is written for one: setup_inputs(seed, part) draws one part's arguments, and reference() takes and returns one part's arrays. A program takes and returns all parts, laid end to end along the dimension named above; each array names one. Nothing has to cross between parts.
Inputs may be any that keep to these rules, and one draw needn't show every extreme that they name: `band_cols`: row block i belongs to col group c = i // 16; each of its tiles lies in a column block of col group c - 1, c or c + 1 taken cyclically, group g holding column blocks g * 2 to (g + 1) * 2 - 1. Tile 0 of row block i is column block c * 2 + (i mod 2). `demand`: positive. `cost`: positive. `bound_type`: 0: lower bound 0 only; 1: between 0 and upper; 2: free.
All inputs are finite; a program needn't handle non-finite values.
Results may differ from the reference program's by a relative error of at most 0.00092.
Values may be sent and summed in bfloat16 or wider, within the bound.
A program may use at most 64 MiB of HBM per device.

```python
import math
import jax
import jax.numpy as jnp
from jax import lax

BLK = 128
SCEN = 256
LEVELS = 16
BAND = 10
ITERS = 2
GROUP = 2
RB = 64
CB = 8
NROW = 8192
NCOL = 1024
N_COL = 4


def draw_band_cols(key, part):
    key = jax.random.fold_in(key, 7)
    first_key, second_key = jax.random.split(key)
    col_count = CB // GROUP
    row_ids = jnp.arange(RB, dtype=jnp.int32)
    owner = row_ids // (RB // col_count)
    column = jnp.arange(BAND, dtype=jnp.int32)[None, :]
    shifts = jax.random.randint(first_key, (RB, BAND), -1, 2, dtype=jnp.int32)
    within = jax.random.randint(second_key, (RB, BAND), 0, GROUP, dtype=jnp.int32)
    shifts = jnp.where(column == 0, 0, shifts)
    within = jnp.where(column == 0, (row_ids % GROUP)[:, None], within)
    return ((owner[:, None] + shifts + col_count) % col_count * GROUP + within).astype(jnp.int32)


def draw_demand(key, part):
    key = jax.random.fold_in(key, 13)
    first_key = jax.random.fold_in(key, 0)
    ramp = 1.0 + 2.0 * jnp.arange(NROW, dtype=jnp.float32) / (NROW - 1)
    return ramp[:, None] * jax.random.uniform(first_key, (NROW, LEVELS), jnp.float32, 0.5, 1.5)


def draw_cost(key, part):
    key = jax.random.fold_in(key, 29)
    first_key = jax.random.fold_in(key, 0)
    ramp = 1.0 + 2.0 * jnp.arange(NCOL, dtype=jnp.float32) / (NCOL - 1)
    return ramp * jax.random.uniform(first_key, (NCOL,), jnp.float32, 0.2, 1.5)


def set_ends(array, own_key, low, top_value):
    spot = [jax.random.randint(jax.random.fold_in(own_key, axis), (), 0, length) for axis, length in enumerate(array.shape)]
    widest = array.shape.index(max(array.shape))
    beside = spot[:widest] + [(spot[widest] + 1) % array.shape[widest]] + spot[widest + 1:]
    return array.at[tuple(spot)].set(low).at[tuple(beside)].set(top_value)


def level_of(stream_key, dims, pieces, low, high):
    def one(axis_at, shards_of):
        heights = jax.random.uniform(jax.random.fold_in(jax.random.fold_in(stream_key, 6), axis_at), (shards_of,), jnp.float32, low / len(pieces), high / len(pieces))
        return jnp.repeat(jnp.exp(heights), dims[axis_at] // shards_of).reshape((-1,) + (1,) * (len(dims) - axis_at - 1))

    level = one(*pieces[0])
    for cut in pieces[1:]:
        level = level * one(*cut)
    return level


def bell_draw(rng, shape, width, reach, cuts=(), kind=jnp.bfloat16):
    values = width * jax.random.normal(rng, shape, jnp.float32)
    if cuts:
        values = values * level_of(rng, shape, cuts, -0.22, 0.18)
    return jnp.clip(values, -reach, reach).astype(kind)


def setup_inputs(seed: int = 0, part: int = 0) -> dict:
    key_of = jax.random.split(jax.random.key(seed), 10)
    own_keys = jax.random.split(jax.random.fold_in(key_of[9], part), 10)
    matrix = bell_draw(own_keys[0], (RB, BAND, BLK, BLK), (BAND * BLK) ** -0.5, 0.15625, ((0, 8),))
    band_cols = draw_band_cols(jax.random.fold_in(jax.random.fold_in(key_of[9], part), 71), part)
    x_start = bell_draw(own_keys[2], (NCOL, SCEN), 1.0, 6.0, ((0, 8), (1, 2)), jnp.float32)
    y_start = jnp.clip(1.0 * jax.random.uniform(own_keys[3], (NROW, SCEN), jnp.float32) ** level_of(own_keys[3], (NROW, SCEN), ((0, 8), (1, 2)), -0.2, 0.2), 0.0, 1.0)
    demand = draw_demand(jax.random.fold_in(jax.random.fold_in(key_of[9], part), 71), part)
    scen_level = set_ends(jax.random.randint(own_keys[5], (SCEN,), 0, LEVELS), jax.random.fold_in(own_keys[5], 1), 0, LEVELS - 1).astype(jnp.int32)
    cost = draw_cost(jax.random.fold_in(jax.random.fold_in(key_of[9], part), 71), part)
    upper = jnp.clip(jnp.exp(math.log(2.0) - 2.3025851 * jax.random.uniform(own_keys[7], (NCOL,), jnp.float32) ** level_of(own_keys[7], (NCOL,), ((0, 8),), -0.2, 0.2)), 0.2, 2.0)
    bound_type = set_ends(jax.random.randint(own_keys[8], (NCOL,), 0, 3), jax.random.fold_in(own_keys[8], 1), 0, 2).astype(jnp.int32)
    return {"matrix": matrix, "band_cols": band_cols, "x_start": x_start, "y_start": y_start, "demand": demand, "scen_level": scen_level, "cost": cost, "upper": upper, "bound_type": bound_type}


step_primal = 0.3
step_dual = 0.3
eps = 1e-06

def clamp_box(value, upper, bound_type):
    lower_only = jnp.maximum(value, 0.0)
    boxed = jnp.minimum(lower_only, upper[:, None])
    return jnp.where(bound_type[:, None] == 0, lower_only, jnp.where(bound_type[:, None] == 1, boxed, value))

def forward_all(matrix, band_cols, extrapolated):
    band_size = matrix.shape[1]
    block_size = matrix.shape[2]
    panel_width = extrapolated.shape[1]
    blocks = extrapolated.reshape(-1, block_size, panel_width)
    batch_count = N_COL
    tile_sets = matrix.reshape(batch_count, -1, band_size, block_size, block_size)
    picked_sets = band_cols.reshape(batch_count, -1, band_size)

    def apply_batch(batch_pair):
        tile_set, picked = batch_pair
        gathered = blocks[picked].astype(jnp.float32)
        return jnp.einsum('ikab,ikbs->ias', tile_set.astype(jnp.float32), gathered)
    results = lax.map(apply_batch, (tile_sets, picked_sets))
    return results.reshape(-1, panel_width)

def backward_all(matrix, band_cols, dual_half):
    band_size = matrix.shape[1]
    block_size = matrix.shape[2]
    panel_width = dual_half.shape[1]
    batch_count = N_COL
    tile_sets = matrix.reshape(batch_count, -1, band_size, block_size, block_size)
    picked_sets = band_cols.reshape(batch_count, -1, band_size)
    dual_sets = dual_half.reshape(batch_count, -1, block_size, panel_width)

    def accumulate(carry, batch_three):
        tile_set, picked, dual_part = batch_three
        contrib = jnp.einsum('ikab,ias->ikbs', tile_set.astype(jnp.float32), dual_part.astype(jnp.float32))
        summed = jax.ops.segment_sum(contrib.reshape(-1, block_size, panel_width), picked.reshape(-1), num_segments=CB)
        return (carry + summed, None)
    start = jnp.zeros((CB, block_size, panel_width), jnp.float32)
    result, _ = lax.scan(accumulate, start, (tile_sets, picked_sets, dual_sets))
    return result.reshape(-1, panel_width)

def reference(matrix, band_cols, x_start, y_start, demand, scen_level, cost, upper, bound_type):
    demand_panel = demand[:, scen_level]
    primal = x_start
    dual = y_start
    scores = []
    for step in range(ITERS):
        pull_back = backward_all(matrix, band_cols, dual.astype(jnp.bfloat16))
        primal_next = clamp_box(primal - step_primal * (cost[:, None] - pull_back), upper, bound_type)
        extrapolated = (2.0 * primal_next - primal).astype(jnp.bfloat16)
        push_forward = forward_all(matrix, band_cols, extrapolated)
        dual_next = jnp.maximum(dual + step_dual * (demand_panel - push_forward), 0.0)
        primal_step = primal_next - primal
        dual_step = dual_next - dual
        primal_score = -lax.optimization_barrier(jnp.sum(cost[:, None] * primal_step, axis=0)) / (NCOL * jnp.sqrt(lax.optimization_barrier(jnp.sum(primal_step * primal_step, axis=0)) / NCOL + eps))
        dual_score = lax.optimization_barrier(jnp.sum(demand_panel * dual_step, axis=0)) / (NROW * jnp.sqrt(lax.optimization_barrier(jnp.sum(dual_step * dual_step, axis=0)) / NROW + eps))
        scores.append(primal_score)
        scores.append(dual_score)
        primal = primal_next
        dual = dual_next
    return (primal, dual, jnp.stack(scores))
```

```python
import functools

import jax
import jax.numpy as jnp
from jax import lax
from jax.experimental import pallas as pl
from jax.experimental.pallas import tpu as pltpu
from jax.sharding import PartitionSpec as P

ITERS = 2
step_primal = 0.3
step_dual = 0.3
eps = 1e-06
MESH = pl.DeviceIdType.MESH
CHUNK = 32


def dot(a, b):
    return jnp.dot(a, b, preferred_element_type=jnp.float32)


def kernel(C, R, cols_ref, mat_hbm, x_hbm, y_hbm, dem_ref, level_ref, cost_ref, upper_ref, kind_ref,
           x_out, y_out, score_ref,
           mat, hi, lo, xv, yv, panel, dual_t, pbuf, rbuf, xbuf, sums, others,
           mat_sem, in_sem, out_sem, p_send, p_recv, x_send, x_recv, s_send, s_recv):
    row_blocks, band, blk, _ = mat.shape
    rows = row_blocks * blk
    levels = dem_ref.shape[0]
    ci, ri = lax.axis_index("col"), lax.axis_index("row")

    def peer(dc, dr):
        return {"col": lax.rem(ci + dc + C, C), "row": lax.rem(ri + dr, R)}

    peers = [(dc, dr) for dc in range(C) for dr in range(R) if (dc, dr) != (0, 0)]

    y_in = pltpu.make_async_copy(y_hbm, yv, in_sem.at[0])
    x_in = pltpu.make_async_copy(x_hbm, xv, in_sem.at[1])

    def mat_in(i):
        return pltpu.make_async_copy(mat_hbm.at[i], mat.at[i], mat_sem.at[i])

    mat_in(0).start()
    y_in.start()
    x_in.start()
    for i in range(1, row_blocks):
        mat_in(i).start()

    barrier = pltpu.get_barrier_semaphore()
    for dc, dr in peers:
        pl.semaphore_signal(barrier, inc=1, device_id=peer(dc, dr), device_id_type=MESH)

    slot_col = [lax.rem(ci + s - 1 + C, C) * R + w for s in range(3) for w in range(R)]

    def densify(i, carry):
        mat_in(i).wait()
        marks = []
        for k in range(band):
            col = cols_ref[i, k]
            marks.append([jnp.where(col == c, 1.0, 0.0).astype(jnp.float32) for c in slot_col])

        def part(r, carry):
            at = pl.ds(pl.multiple_of(r * CHUNK, CHUNK), CHUNK)
            to = pl.ds(pl.multiple_of(i * blk + r * CHUNK, CHUNK), CHUNK)
            total = [None] * (3 * R)
            for k in range(band):
                tile = mat[i, k, at, :].astype(jnp.float32)
                for j in range(3 * R):
                    term = marks[k][j] * tile
                    total[j] = term if k == 0 else total[j] + term
            for j in range(3 * R):
                s, w = j // R, j % R
                top = total[j].astype(jnp.bfloat16)
                hi[s, to, w * blk:(w + 1) * blk] = top
                lo[s, to, w * blk:(w + 1) * blk] = (total[j] - top.astype(jnp.float32)).astype(jnp.bfloat16)
            return carry

        return lax.fori_loop(0, blk // CHUNK, part, carry)

    lax.fori_loop(0, row_blocks, densify, 0)

    y_in.wait()
    for i in range(row_blocks):
        dual_t[:, i * blk:(i + 1) * blk] = yv[i * blk:(i + 1) * blk, :].T.astype(jnp.bfloat16)
    pl.semaphore_wait(barrier, len(peers))

    def down(t, s, dr):
        w = lax.rem(ri + dr, R)
        return pltpu.make_async_remote_copy(
            src_ref=pbuf.at[t, s, w], dst_ref=rbuf.at[t, s, dr],
            send_sem=p_send.at[t, s, dr], recv_sem=p_recv.at[t, s, dr],
            device_id=peer(s - 1, dr), device_id_type=MESH)

    def up(t, s, dr):
        return pltpu.make_async_remote_copy(
            src_ref=xbuf.at[t, 1, ri], dst_ref=xbuf.at[t, s, ri],
            send_sem=x_send.at[t, s, dr], recv_sem=x_recv.at[t, s, dr],
            device_id=peer(1 - s, dr), device_id_type=MESH)

    def arrival(t, s, dr):
        w = lax.rem(ri - dr + R, R)
        return pltpu.make_async_remote_copy(
            src_ref=xbuf.at[t, 1, ri], dst_ref=xbuf.at[t, s, w],
            send_sem=x_send.at[t, s, dr], recv_sem=x_recv.at[t, s, dr],
            device_id=peer(1 - s, dr), device_id_type=MESH)

    moves = [(s, dr) for s in (0, 2, 1) for dr in range(R) if (s, dr) != (1, 0)]

    for t in range(ITERS):
        d = dual_t[...]
        for s in (0, 2, 1):
            product = dot(d, hi[s]) + dot(d, lo[s])
            for w in range(R):
                pbuf[t, s, w] = product[:, w * blk:(w + 1) * blk]
            for dr in range(R):
                if (s, dr) != (1, 0):
                    down(t, s, dr).start()
        if t == 0:
            x_in.wait()
            rows_of = lax.broadcasted_iota(jnp.int32, (levels, blk), 0)
            pick = jnp.where(rows_of == level_ref[...], 1.0, 0.0).astype(jnp.bfloat16)
            part_1 = dem_ref[...].astype(jnp.bfloat16)
            rest = dem_ref[...] - part_1.astype(jnp.float32)
            part_2 = rest.astype(jnp.bfloat16)
            part_3 = (rest - part_2.astype(jnp.float32)).astype(jnp.bfloat16)
            along = (((0,), (0,)), ((), ()))
            parts = [lax.dot_general(q, pick, along, preferred_element_type=jnp.float32)
                     for q in (part_1, part_2, part_3)]
            panel[...] = parts[0] + (parts[1] + parts[2])
            cost = jnp.broadcast_to(cost_ref[...], (blk, blk)).T
            upper = jnp.broadcast_to(upper_ref[...], (blk, blk)).T
            kind = jnp.broadcast_to(kind_ref[...], (blk, blk)).astype(jnp.float32).T
        pulled = pbuf[t, 1, ri]
        for s, dr in moves[::-1]:
            down(t, s, dr).wait_recv()
            pulled = pulled + rbuf[t, s, dr]
        primal = xv[...]
        value = primal - step_primal * (cost - pulled.T)
        low = jnp.maximum(value, 0.0)
        primal_next = jnp.where(kind == 0.0, low, jnp.where(kind == 1.0, jnp.minimum(low, upper), value))
        xbuf[t, 1, ri] = (2.0 * primal_next - primal).astype(jnp.bfloat16)
        for s, dr in moves:
            up(t, s, dr).start()
        primal_step = primal_next - primal
        xv[...] = primal_next
        if t == ITERS - 1:
            x_done = pltpu.make_async_copy(xv, x_out, out_sem.at[row_blocks])
            x_done.start()
        sums[4 * t:4 * t + 1, :] = -jnp.sum(cost * primal_step, axis=0, keepdims=True)
        sums[4 * t + 1:4 * t + 2, :] = jnp.sum(primal_step * primal_step, axis=0, keepdims=True)

        accs = [None] * row_blocks
        for s in (1, 0, 2):
            for dr in range(R):
                if (s, dr) != (1, 0):
                    arrival(t, s, dr).wait_recv()
            x = xbuf[t, s].reshape(R * blk, blk)
            for i in range(row_blocks):
                at = slice(i * blk, (i + 1) * blk)
                term = dot(hi[s, at, :], x) + dot(lo[s, at, :], x)
                accs[i] = term if accs[i] is None else accs[i] + term
        along_rows = jnp.zeros((8, blk), jnp.float32)
        squares = jnp.zeros((8, blk), jnp.float32)
        y_done = []
        for i in range(row_blocks):
            at = slice(i * blk, (i + 1) * blk)
            dual = yv[at, :]
            want = panel[at, :]
            dual_next = jnp.maximum(dual + step_dual * (want - accs[i]), 0.0)
            yv[at, :] = dual_next
            if t == ITERS - 1:
                y_done.append(pltpu.make_async_copy(yv.at[at, :], y_out.at[at, :], out_sem.at[i]))
                y_done[-1].start()
            else:
                dual_t[:, at] = dual_next.T.astype(jnp.bfloat16)
            dual_step = dual_next - dual
            along_rows += jnp.sum((want * dual_step).reshape(-1, 8, blk), axis=0)
            squares += jnp.sum((dual_step * dual_step).reshape(-1, 8, blk), axis=0)
        sums[4 * t + 2:4 * t + 3, :] = jnp.sum(along_rows, axis=0, keepdims=True)
        sums[4 * t + 3:4 * t + 4, :] = jnp.sum(squares, axis=0, keepdims=True)

    def share(n):
        return pltpu.make_async_remote_copy(
            src_ref=sums, dst_ref=others.at[n], send_sem=s_send.at[n], recv_sem=s_recv.at[n],
            device_id=peer(*peers[n]), device_id_type=MESH)

    for n in range(len(peers)):
        share(n).start()
    total = sums[...]
    for n in range(len(peers)):
        share(n).wait_recv()
        total = total + others[n]
    col_total = float(C * R * blk)
    row_total = float(C * R * rows)
    for t in range(ITERS):
        score_ref[2 * t:2 * t + 1, :] = total[4 * t:4 * t + 1, :] / (
            col_total * jnp.sqrt(total[4 * t + 1:4 * t + 2, :] / col_total + eps))
        score_ref[2 * t + 1:2 * t + 2, :] = total[4 * t + 2:4 * t + 3, :] / (
            row_total * jnp.sqrt(total[4 * t + 3:4 * t + 4, :] / row_total + eps))
    for t in range(ITERS):
        for s, dr in moves:
            down(t, s, dr).wait_send()
            up(t, s, dr).wait_send()
    for n in range(len(peers)):
        share(n).wait_send()
    x_done.wait()
    for copy in y_done:
        copy.wait()


def solution(mesh):
    C, R = mesh.shape["col"], mesh.shape["row"]

    def on_device(matrix, band_cols, x_start, y_start, demand, scen_level, cost, upper, bound_type):
        row_blocks, band, blk, _ = matrix.shape
        rows, width = y_start.shape
        f32, bf16 = jnp.float32, jnp.bfloat16
        n_peers = C * R - 1
        dma = pltpu.SemaphoreType.DMA
        vmem = pl.BlockSpec(memory_space=pltpu.VMEM)
        anywhere = pl.BlockSpec(memory_space=pl.ANY)
        return pl.pallas_call(
            functools.partial(kernel, C, R),
            out_shape=(
                jax.ShapeDtypeStruct(x_start.shape, f32),
                jax.ShapeDtypeStruct(y_start.shape, f32),
                jax.ShapeDtypeStruct((2 * ITERS, width), f32),
            ),
            in_specs=[pl.BlockSpec(memory_space=pltpu.SMEM), anywhere, anywhere, anywhere,
                      vmem, vmem, vmem, vmem, vmem],
            out_specs=(anywhere, anywhere, vmem),
            scratch_shapes=[
                pltpu.VMEM(matrix.shape, bf16),
                pltpu.VMEM((3, rows, R * blk), bf16),
                pltpu.VMEM((3, rows, R * blk), bf16),
                pltpu.VMEM(x_start.shape, f32),
                pltpu.VMEM(y_start.shape, f32),
                pltpu.VMEM((rows, width), f32),
                pltpu.VMEM((width, rows), bf16),
                pltpu.VMEM((ITERS, 3, R, width, blk), f32),
                pltpu.VMEM((ITERS, 3, R, width, blk), f32),
                pltpu.VMEM((ITERS, 3, R, blk, width), bf16),
                pltpu.VMEM((4 * ITERS, width), f32),
                pltpu.VMEM((n_peers, 4 * ITERS, width), f32),
                dma((row_blocks,)),
                dma((2,)),
                dma((row_blocks + 1,)),
                dma((ITERS, 3, R)),
                dma((ITERS, 3, R)),
                dma((ITERS, 3, R)),
                dma((ITERS, 3, R)),
                dma((n_peers,)),
                dma((n_peers,)),
            ],
            compiler_params=pltpu.CompilerParams(
                collective_id=0, has_side_effects=True, vmem_limit_bytes=48 * 1024 * 1024
            ),
        )(band_cols, matrix, x_start, y_start, demand.T, scen_level.reshape(1, -1),
          cost.reshape(1, -1), upper.reshape(1, -1), bound_type.reshape(1, -1))

    placed = (
        P(("lp", "col", "row"), None, None, None),
        P(("lp", "col", "row"), None),
        P(("lp", "col", "row"), "sub"),
        P(("lp", "col", "row"), "sub"),
        P(("lp", "col", "row"), None),
        P(("lp", "sub")),
        P(("lp", "col", "row")),
        P(("lp", "col", "row")),
        P(("lp", "col", "row")),
    )
    return jax.shard_map(
        on_device,
        mesh=mesh,
        in_specs=placed,
        out_specs=(
            P(("lp", "col", "row"), "sub"),
            P(("lp", "col", "row"), "sub"),
            P(None, ("lp", "sub")),
        ),
        check_vma=False,
    )
```

```python
import functools

import jax
import jax.numpy as jnp
from jax import lax
from jax.experimental import pallas as pl
from jax.experimental.pallas import tpu as pltpu
from jax.sharding import PartitionSpec as P

ITERS = 2
step_primal = 0.3
step_dual = 0.3
eps = 1e-06
MESH = pl.DeviceIdType.MESH
CHUNK = 32
EXTRA = 16


def coded(block):
    most = jnp.max(jnp.abs(block), axis=0, keepdims=True)
    power = jnp.ceil(jnp.log2(jnp.maximum(most, 1e-30)))
    units = jnp.minimum(jnp.round(block * jnp.exp2(15.0 - power)), 32767.0)
    powers = jnp.broadcast_to(power, (EXTRA, block.shape[1]))
    return jnp.concatenate([units, powers], axis=0).astype(jnp.int32).astype(jnp.int16)


def decoded(message):
    values = message.astype(jnp.int32).astype(jnp.float32)
    return values[:-EXTRA] * jnp.exp2(values[-EXTRA:][:1] - 15.0)


def dot(a, b):
    return jnp.dot(a, b, preferred_element_type=jnp.float32)


def kernel(C, R, cols_hbm, mat_hbm, x_hbm, y_hbm, dem_hbm, level_hbm, cost_hbm, upper_hbm, kind_hbm,
           x_out, y_out, score_ref,
           cols_ref, dem_ref, level_ref, cost_ref, upper_ref, kind_ref, mat, hi, lo, own, xv, yv, panel, dual_t, pbuf, rbuf, xbuf, sums, others,
           mat_sem, in_sem, out_sem, p_send, p_recv, x_send, x_recv, s_send, s_recv):
    row_blocks, band, blk, _ = mat.shape
    rows = row_blocks * blk
    levels = dem_ref.shape[0]
    ci, ri = lax.axis_index("col"), lax.axis_index("row")

    def ring(at, by, size):
        at = at + by % size
        return jnp.where(at >= size, at - size, at)

    def peer(dc, dr):
        return {"col": ring(ci, dc, C), "row": ring(ri, dr, R)}

    peers = [(dc, dr) for dc in range(C) for dr in range(R) if (dc, dr) != (0, 0)]

    barrier = pltpu.get_barrier_semaphore()
    for dc, dr in peers:
        pl.semaphore_signal(barrier, inc=1, device_id=peer(dc, dr), device_id_type=MESH)

    y_in = pltpu.make_async_copy(y_hbm, yv, in_sem.at[0])
    x_in = pltpu.make_async_copy(x_hbm, xv, in_sem.at[1])

    small_in = [
        pltpu.make_async_copy(a, b, in_sem.at[2 + n]) for n, (a, b) in enumerate((
            (cols_hbm, cols_ref), (dem_hbm, dem_ref), (level_hbm, level_ref),
            (cost_hbm, cost_ref), (upper_hbm, upper_ref), (kind_hbm, kind_ref)))]

    def mat_in(i):
        return pltpu.make_async_copy(mat_hbm.at[i], mat.at[i], mat_sem.at[i])

    small_in[0].start()
    mat_in(0).start()
    y_in.start()
    x_in.start()
    for i in range(1, row_blocks):
        mat_in(i).start()
    for copy in small_in[1:]:
        copy.start()

    slot_col = [ring(ci, s - 1, C) * R + w for s in range(3) for w in range(R)]

    small_in[0].wait()

    def densify(i, carry):
        mat_in(i).wait()
        marks = []
        for k in range(band):
            col = cols_ref[i, k]
            marks.append([jnp.where(col == c, 1.0, 0.0).astype(jnp.float32) for c in slot_col])

        def part(r, carry):
            at = pl.ds(pl.multiple_of(r * CHUNK, CHUNK), CHUNK)
            to = pl.ds(pl.multiple_of(i * blk + r * CHUNK, CHUNK), CHUNK)
            total = [None] * (3 * R)
            for k in range(band):
                tile = mat[i, k, at, :].astype(jnp.float32)
                for j in range(3 * R):
                    term = marks[k][j] * tile
                    total[j] = term if k == 0 else total[j] + term
            for j in range(3 * R):
                s, w = j // R, j % R
                top = total[j].astype(jnp.bfloat16)
                hi[s, to, w * blk:(w + 1) * blk] = top
                lo[s, to, w * blk:(w + 1) * blk] = (total[j] - top.astype(jnp.float32)).astype(jnp.bfloat16)
            return carry

        return lax.fori_loop(0, blk // CHUNK, part, carry)

    lax.fori_loop(0, row_blocks, densify, 0)

    y_in.wait()
    for i in range(row_blocks):
        dual_t[:, i * blk:(i + 1) * blk] = yv[i * blk:(i + 1) * blk, :].T.astype(jnp.bfloat16)
    pl.semaphore_wait(barrier, len(peers))

    def down(t, s, dr):
        w = ring(ri, dr, R)
        return pltpu.make_async_remote_copy(
            src_ref=pbuf.at[t, s, w], dst_ref=rbuf.at[t, s, dr],
            send_sem=p_send.at[t, s, dr], recv_sem=p_recv.at[t, s, dr],
            device_id=peer(s - 1, dr), device_id_type=MESH)

    def up(t, s, dr):
        return pltpu.make_async_remote_copy(
            src_ref=xbuf.at[t, 1, ri], dst_ref=xbuf.at[t, s, ri],
            send_sem=x_send.at[t, s, dr], recv_sem=x_recv.at[t, s, dr],
            device_id=peer(1 - s, dr), device_id_type=MESH)

    def arrival(t, s, dr):
        w = ring(ri, -dr, R)
        return pltpu.make_async_remote_copy(
            src_ref=xbuf.at[t, 1, ri], dst_ref=xbuf.at[t, s, w],
            send_sem=x_send.at[t, s, dr], recv_sem=x_recv.at[t, s, dr],
            device_id=peer(1 - s, dr), device_id_type=MESH)

    moves = [(s, dr) for s in (0, 2, 1) for dr in range(R) if (s, dr) != (1, 0)]

    for t in range(ITERS):
        d = dual_t[...]
        for s in (0, 2, 1):
            product = dot(d, hi[s]) + dot(d, lo[s])
            for w in range(R):
                block = product[:, w * blk:(w + 1) * blk]
                if s == 1:
                    own[w] = block
                pbuf[t, s, w] = coded(block)
            for dr in range(R):
                if (s, dr) != (1, 0):
                    down(t, s, dr).start()
        if t == 0:
            x_in.wait()
            for copy in small_in[1:]:
                copy.wait()
            rows_of = lax.broadcasted_iota(jnp.int32, (levels, blk), 0)
            pick = jnp.where(rows_of == level_ref[...], 1.0, 0.0).astype(jnp.bfloat16)
            part_1 = dem_ref[...].astype(jnp.bfloat16)
            rest = dem_ref[...] - part_1.astype(jnp.float32)
            part_2 = rest.astype(jnp.bfloat16)
            part_3 = (rest - part_2.astype(jnp.float32)).astype(jnp.bfloat16)
            along = (((0,), (0,)), ((), ()))
            parts = [lax.dot_general(q, pick, along, preferred_element_type=jnp.float32)
                     for q in (part_1, part_2, part_3)]
            panel[...] = parts[0] + (parts[1] + parts[2])
            cost = jnp.broadcast_to(cost_ref[...], (blk, blk)).T
            upper = jnp.broadcast_to(upper_ref[...], (blk, blk)).T
            kind = jnp.broadcast_to(kind_ref[...], (blk, blk)).astype(jnp.float32).T
        pulled = own[ri]
        for s, dr in moves[::-1]:
            down(t, s, dr).wait_recv()
            pulled = pulled + decoded(rbuf[t, s, dr])
        primal = xv[...]
        value = primal - step_primal * (cost - pulled.T)
        low = jnp.maximum(value, 0.0)
        primal_next = jnp.where(kind == 0.0, low, jnp.where(kind == 1.0, jnp.minimum(low, upper), value))
        xbuf[t, 1, ri] = (2.0 * primal_next - primal).astype(jnp.bfloat16)
        for s, dr in moves:
            up(t, s, dr).start()
        primal_step = primal_next - primal
        xv[...] = primal_next
        if t == ITERS - 1:
            x_done = pltpu.make_async_copy(xv, x_out, out_sem.at[row_blocks])
            x_done.start()
        sums[4 * t:4 * t + 1, :] = -jnp.sum(cost * primal_step, axis=0, keepdims=True)
        sums[4 * t + 1:4 * t + 2, :] = jnp.sum(primal_step * primal_step, axis=0, keepdims=True)

        accs = [None] * row_blocks
        for s in (1, 0, 2):
            for dr in range(R):
                if (s, dr) != (1, 0):
                    arrival(t, s, dr).wait_recv()
            x = xbuf[t, s].reshape(R * blk, blk)
            for i in range(row_blocks):
                at = slice(i * blk, (i + 1) * blk)
                term = dot(hi[s, at, :], x) + dot(lo[s, at, :], x)
                accs[i] = term if accs[i] is None else accs[i] + term
        along_rows = jnp.zeros((8, blk), jnp.float32)
        squares = jnp.zeros((8, blk), jnp.float32)
        y_done = []
        for i in range(row_blocks):
            at = slice(i * blk, (i + 1) * blk)
            dual = yv[at, :]
            want = panel[at, :]
            dual_next = jnp.maximum(dual + step_dual * (want - accs[i]), 0.0)
            yv[at, :] = dual_next
            if t == ITERS - 1:
                y_done.append(pltpu.make_async_copy(yv.at[at, :], y_out.at[at, :], out_sem.at[i]))
                y_done[-1].start()
            else:
                dual_t[:, at] = dual_next.T.astype(jnp.bfloat16)
            dual_step = dual_next - dual
            along_rows += jnp.sum((want * dual_step).reshape(-1, 8, blk), axis=0)
            squares += jnp.sum((dual_step * dual_step).reshape(-1, 8, blk), axis=0)
        sums[4 * t + 2:4 * t + 3, :] = jnp.sum(along_rows, axis=0, keepdims=True)
        sums[4 * t + 3:4 * t + 4, :] = jnp.sum(squares, axis=0, keepdims=True)

    def share(n):
        return pltpu.make_async_remote_copy(
            src_ref=sums, dst_ref=others.at[n], send_sem=s_send.at[n], recv_sem=s_recv.at[n],
            device_id=peer(*peers[n]), device_id_type=MESH)

    for n in range(len(peers)):
        share(n).start()
    total = sums[...]
    for n in range(len(peers)):
        share(n).wait_recv()
        total = total + others[n]
    col_total = float(C * R * blk)
    row_total = float(C * R * rows)
    for t in range(ITERS):
        score_ref[2 * t:2 * t + 1, :] = total[4 * t:4 * t + 1, :] / (
            col_total * jnp.sqrt(total[4 * t + 1:4 * t + 2, :] / col_total + eps))
        score_ref[2 * t + 1:2 * t + 2, :] = total[4 * t + 2:4 * t + 3, :] / (
            row_total * jnp.sqrt(total[4 * t + 3:4 * t + 4, :] / row_total + eps))
    for t in range(ITERS):
        for s, dr in moves:
            down(t, s, dr).wait_send()
            up(t, s, dr).wait_send()
    for n in range(len(peers)):
        share(n).wait_send()
    x_done.wait()
    for copy in y_done:
        copy.wait()


def store(x_ref, y_ref, score_ref, x_out, y_out, score_out, x_at, y_at, score_at, sem):
    part = y_ref.shape[0] // 4
    trips = [(r.at[i * part:(i + 1) * part], y_at.at[i * part:(i + 1) * part], o.at[i * part:(i + 1) * part])
             for i in range(4) for r, o in [(y_ref, y_out)]]
    trips += [(x_ref, x_at, x_out), (score_ref, score_at, score_out)]
    loads = [pltpu.make_async_copy(a, b, sem.at[0, n]) for n, (a, b, _) in enumerate(trips)]
    stores = [pltpu.make_async_copy(b, c, sem.at[1, n]) for n, (_, b, c) in enumerate(trips)]
    for copy in loads:
        copy.start()
    for load, copy in zip(loads, stores):
        load.wait()
        copy.start()
    for copy in stores:
        copy.wait()


def solution(mesh):
    C, R = mesh.shape["col"], mesh.shape["row"]

    def on_device(matrix, band_cols, x_start, y_start, demand, scen_level, cost, upper, bound_type):
        row_blocks, band, blk, _ = matrix.shape
        rows, width = y_start.shape
        f32, bf16 = jnp.float32, jnp.bfloat16
        n_peers = C * R - 1
        dma = pltpu.SemaphoreType.DMA
        vmem = pl.BlockSpec(memory_space=pltpu.VMEM)
        anywhere = pl.BlockSpec(memory_space=pl.ANY)
        shapes = (
            jax.ShapeDtypeStruct(x_start.shape, f32),
            jax.ShapeDtypeStruct(y_start.shape, f32),
            jax.ShapeDtypeStruct((2 * ITERS, width), f32),
        )
        results = pl.pallas_call(
            functools.partial(kernel, C, R),
            out_shape=shapes,
            in_specs=[pl.BlockSpec(memory_space=pltpu.HBM)] * 9,
            out_specs=(anywhere, anywhere, vmem),
            scratch_shapes=[
                pltpu.SMEM(band_cols.shape, jnp.int32),
                pltpu.VMEM(demand.shape[::-1], f32),
                pltpu.VMEM((1, width), jnp.int32),
                pltpu.VMEM((1, blk), f32),
                pltpu.VMEM((1, blk), f32),
                pltpu.VMEM((1, blk), jnp.int32),
                pltpu.VMEM(matrix.shape, bf16),
                pltpu.VMEM((3, rows, R * blk), bf16),
                pltpu.VMEM((3, rows, R * blk), bf16),
                pltpu.VMEM((R, width, blk), f32),
                pltpu.VMEM(x_start.shape, f32),
                pltpu.VMEM(y_start.shape, f32),
                pltpu.VMEM((rows, width), f32),
                pltpu.VMEM((width, rows), bf16),
                pltpu.VMEM((ITERS, 3, R, width + EXTRA, blk), jnp.int16),
                pltpu.VMEM((ITERS, 3, R, width + EXTRA, blk), jnp.int16),
                pltpu.VMEM((ITERS, 3, R, blk, width), bf16),
                pltpu.VMEM((4 * ITERS, width), f32),
                pltpu.VMEM((n_peers, 4 * ITERS, width), f32),
                dma((row_blocks,)),
                dma((8,)),
                dma((row_blocks + 1,)),
                dma((ITERS, 3, R)),
                dma((ITERS, 3, R)),
                dma((ITERS, 3, R)),
                dma((ITERS, 3, R)),
                dma((n_peers,)),
                dma((n_peers,)),
            ],
            compiler_params=pltpu.CompilerParams(
                collective_id=0, has_side_effects=True, vmem_limit_bytes=62 * 1024 * 1024
            ),
        )(band_cols, matrix, x_start, y_start, demand.T, scen_level.reshape(1, -1),
          cost.reshape(1, -1), upper.reshape(1, -1), bound_type.reshape(1, -1))
        return pl.pallas_call(
            store,
            out_shape=shapes,
            in_specs=[anywhere] * 3,
            out_specs=(anywhere,) * 3,
            scratch_shapes=[pltpu.VMEM(q.shape, f32) for q in shapes] + [dma((2, 6))],
            compiler_params=pltpu.CompilerParams(vmem_limit_bytes=62 * 1024 * 1024),
        )(*results)

    placed = (
        P(("lp", "col", "row"), None, None, None),
        P(("lp", "col", "row"), None),
        P(("lp", "col", "row"), "sub"),
        P(("lp", "col", "row"), "sub"),
        P(("lp", "col", "row"), None),
        P(("lp", "sub")),
        P(("lp", "col", "row")),
        P(("lp", "col", "row")),
        P(("lp", "col", "row")),
    )
    return jax.shard_map(
        on_device,
        mesh=mesh,
        in_specs=placed,
        out_specs=(
            P(("lp", "col", "row"), "sub"),
            P(("lp", "col", "row"), "sub"),
            P(None, ("lp", "sub")),
        ),
        check_vma=False,
    )
```

```python
import functools

import jax
import jax.numpy as jnp
from jax import lax
from jax.experimental import pallas as pl
from jax.experimental.pallas import tpu as pltpu
from jax.sharding import PartitionSpec as P

ITERS = 2
step_primal = 0.3
step_dual = 0.3
eps = 1e-06
MESH = pl.DeviceIdType.MESH
CHUNK = 64
EXTRA = 16


def coded(block):
    most = jnp.max(jnp.abs(block), axis=0, keepdims=True)
    power = jnp.ceil(jnp.log2(jnp.maximum(most, 1e-30)))
    units = jnp.minimum(jnp.round(block * jnp.exp2(15.0 - power)), 32767.0)
    powers = jnp.broadcast_to(power, (EXTRA, block.shape[1]))
    return jnp.concatenate([units, powers], axis=0).astype(jnp.int32).astype(jnp.int16)


def decoded(message):
    values = message.astype(jnp.int32).astype(jnp.float32)
    return values[:-EXTRA] * jnp.exp2(values[-EXTRA:][:1] - 15.0)


def dot(a, b):
    return jnp.dot(a, b, preferred_element_type=jnp.float32)


def kernel(C, R, cols_hbm, mat_hbm, x_hbm, y_hbm, dem_hbm, level_hbm, cost_hbm, upper_hbm, kind_hbm,
           x_out, y_out, score_ref,
           cols_ref, dem_ref, level_ref, cost_ref, upper_ref, kind_ref, mat, hi, lo, own, xv, yv, panel, dual_t, pbuf, rbuf, xbuf, sums, others,
           mat_sem, in_sem, out_sem, p_send, p_recv, x_send, x_recv, s_send, s_recv):
    row_blocks, band, blk, _ = mat.shape
    rows = row_blocks * blk
    levels = dem_ref.shape[0]
    ci, ri = lax.axis_index("col"), lax.axis_index("row")

    def ring(at, by, size):
        at = at + by % size
        return jnp.where(at >= size, at - size, at)

    def peer(dc, dr):
        return {"col": ring(ci, dc, C), "row": ring(ri, dr, R)}

    peers = [(dc, dr) for dc in range(C) for dr in range(R) if (dc, dr) != (0, 0)]

    barrier = pltpu.get_barrier_semaphore()
    for dc, dr in peers:
        pl.semaphore_signal(barrier, inc=1, device_id=peer(dc, dr), device_id_type=MESH)

    y_in = pltpu.make_async_copy(y_hbm, yv, in_sem.at[0])
    x_in = pltpu.make_async_copy(x_hbm, xv, in_sem.at[1])

    small_in = [
        pltpu.make_async_copy(a, b, in_sem.at[2 + n]) for n, (a, b) in enumerate((
            (cols_hbm, cols_ref), (dem_hbm, dem_ref), (level_hbm, level_ref),
            (cost_hbm, cost_ref), (upper_hbm, upper_ref), (kind_hbm, kind_ref)))]

    def mat_in(i):
        return pltpu.make_async_copy(mat_hbm.at[i], mat.at[i], mat_sem.at[i])

    small_in[0].start()
    mat_in(0).start()
    y_in.start()
    x_in.start()
    for i in range(1, row_blocks):
        mat_in(i).start()
    for copy in small_in[1:]:
        copy.start()

    slot_col = [ring(ci, s - 1, C) * R + w for s in range(3) for w in range(R)]

    small_in[0].wait()

    def densify(s, first):
        def one(i, carry):
            if first:
                mat_in(i).wait()
            marks = []
            for k in range(band):
                col = cols_ref[i, k]
                marks.append([jnp.where(col == c, 1.0, 0.0).astype(jnp.float32) for c in slot_col[s * R:(s + 1) * R]])

            def part(r, carry):
                at = pl.ds(pl.multiple_of(r * CHUNK, CHUNK), CHUNK)
                to = pl.ds(pl.multiple_of(i * blk + r * CHUNK, CHUNK), CHUNK)
                total = [None] * R
                for k in range(band):
                    tile = mat[i, k, at, :].astype(jnp.float32)
                    for w in range(R):
                        term = marks[k][w] * tile
                        total[w] = term if k == 0 else total[w] + term
                for w in range(R):
                    top = total[w].astype(jnp.bfloat16)
                    hi[s, to, w * blk:(w + 1) * blk] = top
                    lo[s, to, w * blk:(w + 1) * blk] = (total[w] - top.astype(jnp.float32)).astype(jnp.bfloat16)
                return carry

            return lax.fori_loop(0, blk // CHUNK, part, carry, unroll=True)

        lax.fori_loop(0, row_blocks, one, 0)

    y_in.wait()
    for i in range(row_blocks):
        dual_t[:, i * blk:(i + 1) * blk] = yv[i * blk:(i + 1) * blk, :].T.astype(jnp.bfloat16)

    def down(t, s, dr):
        w = ring(ri, dr, R)
        return pltpu.make_async_remote_copy(
            src_ref=pbuf.at[t, s, w], dst_ref=rbuf.at[t, s, dr],
            send_sem=p_send.at[t, s, dr], recv_sem=p_recv.at[t, s, dr],
            device_id=peer(s - 1, dr), device_id_type=MESH)

    def up(t, s, dr):
        return pltpu.make_async_remote_copy(
            src_ref=xbuf.at[t, 1, ri], dst_ref=xbuf.at[t, s, ri],
            send_sem=x_send.at[t, s, dr], recv_sem=x_recv.at[t, s, dr],
            device_id=peer(1 - s, dr), device_id_type=MESH)

    def arrival(t, s, dr):
        w = ring(ri, -dr, R)
        return pltpu.make_async_remote_copy(
            src_ref=xbuf.at[t, 1, ri], dst_ref=xbuf.at[t, s, w],
            send_sem=x_send.at[t, s, dr], recv_sem=x_recv.at[t, s, dr],
            device_id=peer(1 - s, dr), device_id_type=MESH)

    moves = [(s, dr) for s in (0, 2, 1) for dr in range(R) if (s, dr) != (1, 0)]

    for t in range(ITERS):
        d = dual_t[...]
        for s in (0, 2, 1):
            if t == 0:
                densify(s, s == 0)
            product = dot(d, hi[s]) + dot(d, lo[s])
            for w in range(R):
                block = product[:, w * blk:(w + 1) * blk]
                if s == 1:
                    own[w] = block
                pbuf[t, s, w] = coded(block)
            if (t, s) == (0, 0):
                pl.semaphore_wait(barrier, len(peers))
            for dr in range(R):
                if (s, dr) != (1, 0):
                    down(t, s, dr).start()
        if t == 0:
            x_in.wait()
            for copy in small_in[1:]:
                copy.wait()
            rows_of = lax.broadcasted_iota(jnp.int32, (levels, blk), 0)
            pick = jnp.where(rows_of == level_ref[...], 1.0, 0.0).astype(jnp.bfloat16)
            part_1 = dem_ref[...].astype(jnp.bfloat16)
            rest = dem_ref[...] - part_1.astype(jnp.float32)
            part_2 = rest.astype(jnp.bfloat16)
            part_3 = (rest - part_2.astype(jnp.float32)).astype(jnp.bfloat16)
            along = (((0,), (0,)), ((), ()))
            parts = [lax.dot_general(q, pick, along, preferred_element_type=jnp.float32)
                     for q in (part_1, part_2, part_3)]
            panel[...] = parts[0] + (parts[1] + parts[2])
            cost = jnp.broadcast_to(cost_ref[...], (blk, blk)).T
            upper = jnp.broadcast_to(upper_ref[...], (blk, blk)).T
            kind = jnp.broadcast_to(kind_ref[...], (blk, blk)).astype(jnp.float32).T
        pulled = own[ri]
        for s, dr in moves[::-1]:
            down(t, s, dr).wait_recv()
            pulled = pulled + decoded(rbuf[t, s, dr])
        primal = xv[...]
        value = primal - step_primal * (cost - pulled.T)
        low = jnp.maximum(value, 0.0)
        primal_next = jnp.where(kind == 0.0, low, jnp.where(kind == 1.0, jnp.minimum(low, upper), value))
        xbuf[t, 1, ri] = (2.0 * primal_next - primal).astype(jnp.bfloat16)
        for s, dr in moves:
            up(t, s, dr).start()
        primal_step = primal_next - primal
        xv[...] = primal_next
        if t == ITERS - 1:
            x_done = pltpu.make_async_copy(xv, x_out, out_sem.at[row_blocks])
            x_done.start()
        sums[4 * t:4 * t + 1, :] = -jnp.sum(cost * primal_step, axis=0, keepdims=True)
        sums[4 * t + 1:4 * t + 2, :] = jnp.sum(primal_step * primal_step, axis=0, keepdims=True)

        accs = [None] * row_blocks
        for s in (1, 0, 2):
            for dr in range(R):
                if (s, dr) != (1, 0):
                    arrival(t, s, dr).wait_recv()
            x = xbuf[t, s].reshape(R * blk, blk)
            for i in range(row_blocks):
                at = slice(i * blk, (i + 1) * blk)
                term = dot(hi[s, at, :], x) + dot(lo[s, at, :], x)
                accs[i] = term if accs[i] is None else accs[i] + term
        along_rows = jnp.zeros((8, blk), jnp.float32)
        squares = jnp.zeros((8, blk), jnp.float32)
        y_done = []
        for i in range(row_blocks):
            at = slice(i * blk, (i + 1) * blk)
            dual = yv[at, :]
            want = panel[at, :]
            dual_next = jnp.maximum(dual + step_dual * (want - accs[i]), 0.0)
            yv[at, :] = dual_next
            if t == ITERS - 1:
                y_done.append(pltpu.make_async_copy(yv.at[at, :], y_out.at[at, :], out_sem.at[i]))
                y_done[-1].start()
            else:
                dual_t[:, at] = dual_next.T.astype(jnp.bfloat16)
            dual_step = dual_next - dual
            along_rows += jnp.sum((want * dual_step).reshape(-1, 8, blk), axis=0)
            squares += jnp.sum((dual_step * dual_step).reshape(-1, 8, blk), axis=0)
        sums[4 * t + 2:4 * t + 3, :] = jnp.sum(along_rows, axis=0, keepdims=True)
        sums[4 * t + 3:4 * t + 4, :] = jnp.sum(squares, axis=0, keepdims=True)

    def share(n):
        return pltpu.make_async_remote_copy(
            src_ref=sums, dst_ref=others.at[n], send_sem=s_send.at[n], recv_sem=s_recv.at[n],
            device_id=peer(*peers[n]), device_id_type=MESH)

    for n in range(len(peers)):
        share(n).start()
    total = sums[...]
    for n in range(len(peers)):
        share(n).wait_recv()
        total = total + others[n]
    col_total = float(C * R * blk)
    row_total = float(C * R * rows)
    for t in range(ITERS):
        score_ref[2 * t:2 * t + 1, :] = total[4 * t:4 * t + 1, :] / (
            col_total * jnp.sqrt(total[4 * t + 1:4 * t + 2, :] / col_total + eps))
        score_ref[2 * t + 1:2 * t + 2, :] = total[4 * t + 2:4 * t + 3, :] / (
            row_total * jnp.sqrt(total[4 * t + 3:4 * t + 4, :] / row_total + eps))
    for t in range(ITERS):
        for s, dr in moves:
            down(t, s, dr).wait_send()
            up(t, s, dr).wait_send()
    for n in range(len(peers)):
        share(n).wait_send()
    x_done.wait()
    for copy in y_done:
        copy.wait()


def store(x_ref, y_ref, score_ref, x_out, y_out, score_out, x_at, y_at, score_at, sem):
    part = y_ref.shape[0] // 4
    trips = [(r.at[i * part:(i + 1) * part], y_at.at[i * part:(i + 1) * part], o.at[i * part:(i + 1) * part])
             for i in range(4) for r, o in [(y_ref, y_out)]]
    trips += [(x_ref, x_at, x_out), (score_ref, score_at, score_out)]
    loads = [pltpu.make_async_copy(a, b, sem.at[0, n]) for n, (a, b, _) in enumerate(trips)]
    stores = [pltpu.make_async_copy(b, c, sem.at[1, n]) for n, (_, b, c) in enumerate(trips)]
    for copy in loads:
        copy.start()
    for load, copy in zip(loads, stores):
        load.wait()
        copy.start()
    for copy in stores:
        copy.wait()


def solution(mesh):
    C, R = mesh.shape["col"], mesh.shape["row"]

    def on_device(matrix, band_cols, x_start, y_start, demand, scen_level, cost, upper, bound_type):
        row_blocks, band, blk, _ = matrix.shape
        rows, width = y_start.shape
        f32, bf16 = jnp.float32, jnp.bfloat16
        n_peers = C * R - 1
        dma = pltpu.SemaphoreType.DMA
        vmem = pl.BlockSpec(memory_space=pltpu.VMEM)
        anywhere = pl.BlockSpec(memory_space=pl.ANY)
        shapes = (
            jax.ShapeDtypeStruct(x_start.shape, f32),
            jax.ShapeDtypeStruct(y_start.shape, f32),
            jax.ShapeDtypeStruct((2 * ITERS, width), f32),
        )
        results = pl.pallas_call(
            functools.partial(kernel, C, R),
            out_shape=shapes,
            in_specs=[pl.BlockSpec(memory_space=pltpu.HBM)] * 9,
            out_specs=(anywhere, anywhere, vmem),
            scratch_shapes=[
                pltpu.SMEM(band_cols.shape, jnp.int32),
                pltpu.VMEM(demand.shape[::-1], f32),
                pltpu.VMEM((1, width), jnp.int32),
                pltpu.VMEM((1, blk), f32),
                pltpu.VMEM((1, blk), f32),
                pltpu.VMEM((1, blk), jnp.int32),
                pltpu.VMEM(matrix.shape, bf16),
                pltpu.VMEM((3, rows, R * blk), bf16),
                pltpu.VMEM((3, rows, R * blk), bf16),
                pltpu.VMEM((R, width, blk), f32),
                pltpu.VMEM(x_start.shape, f32),
                pltpu.VMEM(y_start.shape, f32),
                pltpu.VMEM((rows, width), f32),
                pltpu.VMEM((width, rows), bf16),
                pltpu.VMEM((ITERS, 3, R, width + EXTRA, blk), jnp.int16),
                pltpu.VMEM((ITERS, 3, R, width + EXTRA, blk), jnp.int16),
                pltpu.VMEM((ITERS, 3, R, blk, width), bf16),
                pltpu.VMEM((4 * ITERS, width), f32),
                pltpu.VMEM((n_peers, 4 * ITERS, width), f32),
                dma((row_blocks,)),
                dma((8,)),
                dma((row_blocks + 1,)),
                dma((ITERS, 3, R)),
                dma((ITERS, 3, R)),
                dma((ITERS, 3, R)),
                dma((ITERS, 3, R)),
                dma((n_peers,)),
                dma((n_peers,)),
            ],
            compiler_params=pltpu.CompilerParams(
                collective_id=0, has_side_effects=True, vmem_limit_bytes=62 * 1024 * 1024
            ),
        )(band_cols, matrix, x_start, y_start, demand.T, scen_level.reshape(1, -1),
          cost.reshape(1, -1), upper.reshape(1, -1), bound_type.reshape(1, -1))
        return pl.pallas_call(
            store,
            out_shape=shapes,
            in_specs=[anywhere] * 3,
            out_specs=(anywhere,) * 3,
            scratch_shapes=[pltpu.VMEM(q.shape, f32) for q in shapes] + [dma((2, 6))],
            compiler_params=pltpu.CompilerParams(vmem_limit_bytes=62 * 1024 * 1024),
        )(*results)

    placed = (
        P(("lp", "col", "row"), None, None, None),
        P(("lp", "col", "row"), None),
        P(("lp", "col", "row"), "sub"),
        P(("lp", "col", "row"), "sub"),
        P(("lp", "col", "row"), None),
        P(("lp", "sub")),
        P(("lp", "col", "row")),
        P(("lp", "col", "row")),
        P(("lp", "col", "row")),
    )
    return jax.shard_map(
        on_device,
        mesh=mesh,
        in_specs=placed,
        out_specs=(
            P(("lp", "col", "row"), "sub"),
            P(("lp", "col", "row"), "sub"),
            P(None, ("lp", "sub")),
        ),
        check_vma=False,
    )
```
